256 devices in a mesh: row: 16 (over x, y_hi, core), col: 16 (over z, y_lo).
Axes of the slice: x: 4, y: 4 (y_hi: 2, y_lo: 2; y = y_hi * 2 + y_lo), z: 8, core: 2. Of those that a mesh axis runs over, the one named last changes fastest.
Arguments:
- right_side: float32 [65536, 128], P(('row', 'col')), may hold values from -6 to 6
- cov_blocks: bfloat16 [16, 16, 48, 128, 128], P('row', 'col'), as said below
- row_blocks: int32 [16, 16, 48], P('row', 'col'), may hold values from 0 to 31, as said below
- col_blocks: int32 [16, 16, 48], P('row', 'col'), may hold values from 0 to 31, as said below
- block_counts: int32 [16, 16], P('row', 'col'), may hold values from 24 to 48, as said below
Outputs:
- solution_field: float32 [65536, 128], P(('row', 'col'))
- residual: float32 [65536, 128], P(('row', 'col'))
The draws below stay inside these ranges and needn't reach their ends.
Inputs may be any that keep to these rules, and one draw needn't show every extreme that they name: Slots k < 2 of device (a, b) hold the diagonal block of the device's own k-th point block: row_blocks = b*2 + k and col_blocks = a*2 + k; those blocks are symmetric. Other slots name any block; repeated coordinates add. `col_blocks`: as for row_blocks. `block_counts`: some device holds 48 live slots in every draw. `cov_blocks`: the covariance is symmetric positive definite.
All inputs are finite; a program needn't handle non-finite values.
Results may differ from the reference program's by a relative error of at most 0.0003.
Values sent between devices are 32-bit elements; how exact they have to be, the bound alone decides.
No kernel may reach another device: no remote copies, remote signals or barrier semaphores. Data moves between devices by JAX's collectives and lax.ppermute only.
A program may use at most 64 MiB of HBM per device.

```python
import jax
import jax.numpy as jnp
from jax import lax

BLOCK = 128
FIELDS = 128
BD = 2
KB = 48
ITERS = 3
POINTS = 65536
N_ROW = 16
N_COL = 16


def draw_row_blocks(key, part):
    key = jax.random.fold_in(key, 1)
    first, second, third = jax.random.split(key, 3)
    block_values = jax.random.randint(first, (N_ROW, N_COL, KB), 0, BD * N_COL)
    col_group = jnp.arange(N_COL, dtype=jnp.int32)[None, :, None]
    offsets = jax.random.randint(second, (N_ROW, N_COL, KB), -BD, 2 * BD)
    nearby = (col_group * BD + offsets) % (BD * N_COL)
    select_neighbours = jax.random.randint(third, (N_ROW, N_COL, KB), 0, 2)
    block_values = jnp.where(select_neighbours == 1, nearby, block_values)
    slot_index = jnp.arange(KB, dtype=jnp.int32)[None, None, :]
    diagonal_entries = col_group * BD + slot_index + 0 * block_values
    return jnp.where(slot_index < BD, diagonal_entries, block_values).astype(jnp.int32)


def draw_col_blocks(key, part):
    key = jax.random.fold_in(key, 2)
    first, second, third = jax.random.split(key, 3)
    block_values = jax.random.randint(first, (N_ROW, N_COL, KB), 0, BD * N_ROW)
    row_cluster = jnp.arange(N_ROW, dtype=jnp.int32)[:, None, None]
    offsets = jax.random.randint(second, (N_ROW, N_COL, KB), -BD, 2 * BD)
    nearby = (row_cluster * BD + offsets) % (BD * N_ROW)
    select_neighbours = jax.random.randint(third, (N_ROW, N_COL, KB), 0, 2)
    block_values = jnp.where(select_neighbours == 1, nearby, block_values)
    slot_index = jnp.arange(KB, dtype=jnp.int32)[None, None, :]
    diagonal_entries = row_cluster * BD + slot_index + 0 * block_values
    return jnp.where(slot_index < BD, diagonal_entries, block_values).astype(jnp.int32)


def draw_block_counts(key, part):
    key = jax.random.fold_in(key, 3)
    first, second = jax.random.split(key)
    lowest = max(BD, KB // 2)
    block_values = jax.random.randint(first, (N_ROW * N_COL,), lowest, KB + 1)
    chosen = jax.random.randint(second, (), 0, N_ROW * N_COL)
    block_values = jnp.where(jnp.arange(N_ROW * N_COL) == chosen, KB, block_values)
    return block_values.reshape(N_ROW, N_COL).astype(jnp.int32)


def draw_cov_blocks(key, part):
    key = jax.random.fold_in(key, 4)
    first, second = jax.random.split(key)
    shape = (N_ROW, N_COL, KB, BLOCK, BLOCK)
    spread = 0.3 * (BD / (2.0 * KB * BLOCK)) ** 0.5
    noise = jax.random.normal(first, shape, jnp.float32)
    noise = noise * spread
    symmetric = (noise + jnp.swapaxes(noise, -1, -2)) * 0.7071
    heights = jax.random.uniform(second, (N_ROW, N_COL, KB, BLOCK), jnp.float32, 1.0, 2.0)
    identity = jnp.eye(BLOCK, dtype=jnp.float32)
    diagonal_tiles = symmetric + heights[..., None] * identity
    slot_index = jnp.arange(KB)[None, None, :, None, None]
    tiles = jnp.where(slot_index < BD, diagonal_tiles, noise)
    return tiles.astype(jnp.bfloat16)


def block_levels(own_key, extent, shards, least, high):
    factor_of, own = 1.0, jax.random.fold_in(own_key, 6)
    for position, blocks in shards:
        draws = jnp.exp(jax.random.uniform(jax.random.fold_in(own, position), (blocks,), jnp.float32, least / len(shards), high / len(shards)))
        factor_of = factor_of * jnp.repeat(draws, extent[position] // blocks).reshape([-1 if axis == position else 1 for axis in range(len(extent))])
    return factor_of


def scatter_about(key, extent, scale, limit, pieces=(), kind=jnp.bfloat16):
    factor_of = block_levels(key, extent, pieces, -0.22, 0.18) if pieces else 1.0
    drawn = jax.random.normal(key, extent, jnp.float32) * scale * factor_of
    return jnp.minimum(jnp.maximum(drawn, -limit), limit).astype(kind)


def setup_inputs(seed: int = 0) -> dict:
    key_list = jax.random.split(jax.random.key(seed), 6)
    return {
        "right_side": scatter_about(key_list[0], (POINTS, FIELDS), 1.0, 6.0, ((0, 256),), jnp.float32),
        "cov_blocks": draw_cov_blocks(jax.random.fold_in(key_list[5], 71), 0),
        "row_blocks": draw_row_blocks(jax.random.fold_in(key_list[5], 71), 0),
        "col_blocks": draw_col_blocks(jax.random.fold_in(key_list[5], 71), 0),
        "block_counts": draw_block_counts(jax.random.fold_in(key_list[5], 71), 0),
    }


def apply_matrix(vector, cov_blocks, row_blocks, col_blocks, block_counts):
    block_total = vector.shape[0] // BLOCK
    points = vector.reshape(block_total, BLOCK, vector.shape[1])
    slot_index = jnp.arange(KB, dtype=jnp.int32)

    def add_device(totals, device):
        row_cluster = device // N_COL
        col_group = device % N_COL
        tile_values = cov_blocks[row_cluster, col_group].astype(jnp.float32)
        local_rows = row_blocks[row_cluster, col_group]
        local_cols = col_blocks[row_cluster, col_group]
        global_row = row_cluster * (BD * N_COL) + local_rows
        global_col = (local_cols // BD) * (BD * N_COL) + col_group * BD + local_cols % BD
        live_slot = (slot_index < block_counts[row_cluster, col_group]).astype(jnp.float32)
        mirror_live = live_slot * (slot_index >= BD).astype(jnp.float32)
        direct_product = jnp.einsum("kab,kbr->kar", tile_values, points[global_col], precision=lax.Precision.HIGHEST)
        transposed_product = jnp.einsum("kab,kar->kbr", tile_values, points[global_row], precision=lax.Precision.HIGHEST)
        totals = totals.at[global_row].add(direct_product * live_slot[:, None, None])
        totals = totals.at[global_col].add(transposed_product * mirror_live[:, None, None])
        return totals, None

    start = jnp.zeros(points.shape, jnp.float32)
    totals, _ = lax.scan(add_device, start, jnp.arange(N_ROW * N_COL, dtype=jnp.int32))
    return totals.reshape(vector.shape)


def reference(right_side, cov_blocks, row_blocks, col_blocks, block_counts):
    solution_field = jnp.zeros_like(right_side)
    residual = right_side
    direction = right_side
    norm_now = jnp.sum(residual * residual, axis=0)
    for iteration in range(ITERS):
        image = apply_matrix(direction, cov_blocks, row_blocks, col_blocks, block_counts)
        step_size = norm_now / jnp.sum(direction * image, axis=0)
        solution_field = solution_field + step_size * direction
        residual = residual - step_size * image
        norm_next = jnp.sum(residual * residual, axis=0)
        direction = residual + (norm_next / norm_now) * direction
        norm_now = norm_next
    return solution_field, residual
```

```python
import functools

import jax
import jax.numpy as jnp
from jax import lax
from jax.experimental import pallas as pl
from jax.experimental.pallas import tpu as pltpu
from jax.sharding import PartitionSpec as P

NX, NYH, NCORE, NZ, NYL = 4, 2, 2, 8, 2
TILE = 128
OWN = 2
EXTRA = 8
UNROLL = 8


def row_shift(value, dx=0, dyh=0, dcore=0):
    pairs = []
    for r in range(NX * NYH * NCORE):
        x, yh, core = r // 4, (r // 2) % 2, r % 2
        pairs.append((r, ((x + dx) % NX) * 4 + (yh ^ dyh) * 2 + (core ^ dcore)))
    return lax.ppermute(value, "row", pairs)


def col_shift(value, dz=0, dyl=0):
    pairs = []
    for c in range(NZ * NYL):
        z, yl = c // 2, c % 2
        pairs.append((c, ((z + dz) % NZ) * 2 + (yl ^ dyl)))
    return lax.ppermute(value, "col", pairs)


def gather_row(shard):
    pair = jnp.stack([shard, row_shift(shard, dyh=1)])
    near = [pair] + [row_shift(pair, dx=d) for d in (1, 2, 3)]
    return near + [row_shift(piece, dcore=1) for piece in near]


def scatter_row(parts):
    near = [parts[d] + row_shift(parts[NX + d], dcore=1) for d in range(NX)]
    total = near[0]
    for d in (1, 2, 3):
        total = total + row_shift(near[d], dx=d)
    return total[0] + row_shift(total[1], dyh=1)


def gather_col(shard):
    pair = jnp.stack([shard, col_shift(shard, dyl=1)])
    pieces = [pair] * NZ
    up = down = pair
    for d in (1, 2, 3, 4):
        up = col_shift(up, dz=1)
        pieces[d] = up
        if d < 4:
            down = col_shift(down, dz=-1)
            pieces[NZ - d] = down
    return pieces


def scatter_col(parts):
    up = col_shift(parts[4], dz=1) + parts[3]
    down = col_shift(parts[5], dz=-1) + parts[6]
    up = col_shift(up, dz=1) + parts[2]
    down = col_shift(down, dz=-1) + parts[7]
    up = col_shift(up, dz=1) + parts[1]
    down = col_shift(down, dz=-1)
    up = col_shift(up, dz=1)
    total = parts[0] + up + down
    return total[0] + col_shift(total[1], dyl=1)


def split_into(split_ref, block, value):
    high = value.astype(jnp.bfloat16)
    low = (value - high.astype(jnp.float32)).astype(jnp.bfloat16)
    split_ref[block, :, 0:TILE] = high
    split_ref[block, :, TILE:] = low


def product_kernel(pieces, inner, first, contract, rows, *refs):
    source_ref, target_ref, tiles_ref = refs[:3]
    piece_refs = refs[3 : 3 + pieces]
    out_refs = refs[3 + pieces : -2]
    split_ref, total_ref = refs[-2:]
    slots = tiles_ref.shape[0]
    for p in range(pieces):
        for q in range(inner):
            for h in range(OWN):
                block = (p * inner + q) * OWN + h
                split_into(split_ref, block, piece_refs[p][q, h * TILE : (h + 1) * TILE, :])
    total_ref[...] = jnp.zeros_like(total_ref)

    def one(k):
        product = lax.dot_general(
            tiles_ref[k],
            split_ref[source_ref[k]],
            (((contract,), (0,)), ((), ())),
            preferred_element_type=jnp.float32,
        )
        total_ref[target_ref[k]] += product[:, 0:TILE] + product[:, TILE:]

    head = first + (slots - first) % UNROLL
    for k in range(first, head):
        one(k)

    def body(step, carry):
        for u in range(UNROLL):
            one(head + step * UNROLL + u)
        return carry

    lax.fori_loop(0, (slots - head) // UNROLL, body, 0)
    if rows > OWN * TILE:
        extra = jnp.zeros((EXTRA, TILE), jnp.float32)
        for p in range(pieces):
            for q in range(inner):
                extra = extra + piece_refs[p][q, OWN * TILE :, :]
    outs = len(out_refs)
    out_inner = (pieces * inner) // outs
    for p in range(outs):
        for q in range(out_inner):
            for h in range(OWN):
                block = (p * out_inner + q) * OWN + h
                out_refs[p][q, h * TILE : (h + 1) * TILE, :] = total_ref[block]
            if rows > OWN * TILE:
                out_refs[p][q, OWN * TILE :, :] = extra


def products(sources, targets, tiles, pieces, outs, first, contract, rows):
    inner = pieces[0].shape[0]
    count = len(pieces) * inner
    smem = pl.BlockSpec(memory_space=pltpu.SMEM)
    vmem = pl.BlockSpec(memory_space=pltpu.VMEM)
    out_shape = jax.ShapeDtypeStruct((count // outs, rows, TILE), jnp.float32)
    return pl.pallas_call(
        functools.partial(product_kernel, len(pieces), inner, first, contract, rows),
        out_shape=[out_shape] * outs,
        in_specs=[smem, smem] + [vmem] * (1 + len(pieces)),
        out_specs=[vmem] * outs,
        scratch_shapes=[
            pltpu.VMEM((count * OWN, TILE, 2 * TILE), jnp.bfloat16),
            pltpu.VMEM((count * OWN + 1, TILE, TILE), jnp.float32),
        ],
        compiler_params=pltpu.CompilerParams(vmem_limit_bytes=32 * 1024 * 1024),
        cost_estimate=pl.CostEstimate(
            flops=tiles.shape[0] * 4 * TILE**3, bytes_accessed=6 * 1024 * 1024, transcendentals=0
        ),
    )(sources, targets, tiles, *pieces)


def places(row_blocks, col_blocks, block_counts):
    slots = row_blocks.shape[-1]
    row_blocks = row_blocks.reshape(slots)
    col_blocks = col_blocks.reshape(slots)
    r, c = lax.axis_index("row"), lax.axis_index("col")
    x, yh, core = r // 4, (r // 2) % 2, r % 2
    z, yl = c // 2, c % 2
    slot = jnp.arange(slots, dtype=jnp.int32)
    live = slot < block_counts.reshape(())
    device, half = col_blocks // OWN, col_blocks % OWN
    dcore, dyh, ox = core ^ (device % 2), yh ^ ((device // 2) % 2), device // 4
    direct_source = ((dcore * NX + (x - ox) % NX) * NYH + dyh) * OWN + half
    mirror_target = ((dcore * NX + (ox - x) % NX) * NYH + dyh) * OWN + half
    device, half = row_blocks // OWN, row_blocks % OWN
    dyl, oz = yl ^ (device % 2), device // 2
    mirror_source = (((z - oz) % NZ) * NYL + dyl) * OWN + half
    direct_target = (((oz - z) % NZ) * NYL + dyl) * OWN + half
    unused = NX * NYH * NCORE * OWN
    direct_target = jnp.where(live, direct_target, unused)
    mirror_target = jnp.where(live & (slot >= OWN), mirror_target, unused)
    return direct_source, direct_target, mirror_source, mirror_target


def apply_matrix(vector, sums, tiles, where):
    direct_source, direct_target, mirror_source, mirror_target = where
    own = vector.shape[0]
    by_row = gather_row(jnp.concatenate([vector, sums]))
    by_col = gather_col(vector)
    direct = products(direct_source, direct_target, tiles, by_row, NZ, 0, 1, own + EXTRA)
    mirror = products(mirror_source, mirror_target, tiles, by_col, NX * NCORE, OWN, 0, own)
    image = scatter_col(direct)
    return image[:own] + scatter_row(mirror), image[own:]


def column_dots(pairs):
    dots = jnp.stack([jnp.sum(a * b, axis=0) for a, b in pairs])
    return jnp.concatenate([dots, jnp.zeros((EXTRA - len(pairs), dots.shape[1]), jnp.float32)])


def sum_devices(value):
    value = value + row_shift(value, dcore=1)
    value = value + row_shift(value, dyh=1)
    value = value + col_shift(value, dyl=1)
    value = value + row_shift(value, dx=1)
    value = value + row_shift(value, dx=2)
    value = value + col_shift(value, dz=1)
    value = value + col_shift(value, dz=2)
    return value + col_shift(value, dz=4)


def shards(right_side, cov_blocks, row_blocks, col_blocks, block_counts):
    tiles = cov_blocks.reshape(cov_blocks.shape[2:])
    where = places(row_blocks, col_blocks, block_counts)
    apply = functools.partial(apply_matrix, tiles=tiles, where=where)

    r0 = right_side
    w0, _ = apply(r0, jnp.zeros((EXTRA, r0.shape[1]), jnp.float32))
    z0, sums = apply(w0, column_dots([(r0, r0), (w0, r0)]))
    norm0, curvature = sums[0], sums[1]
    alpha0 = norm0 / curvature
    r1 = r0 - alpha0 * w0
    w1 = w0 - alpha0 * z0
    q1, sums = apply(w1, column_dots([(r1, r1), (w1, r1)]))
    norm1 = sums[0]
    beta = norm1 / norm0
    alpha1 = norm1 / (sums[1] - beta * norm1 / alpha0)
    p1 = r1 + beta * r0
    s1 = w1 + beta * w0
    z1 = q1 + beta * z0
    r2 = r1 - alpha1 * s1
    w2 = w1 - alpha1 * z1
    sums = sum_devices(column_dots([(r2, r2), (w2, r2)]))
    norm2 = sums[0]
    beta = norm2 / norm1
    alpha2 = norm2 / (sums[1] - beta * norm2 / alpha1)
    solution_field = alpha0 * r0 + alpha1 * p1 + alpha2 * (r2 + beta * p1)
    residual = r2 - alpha2 * (w2 + beta * s1)
    return (solution_field, residual)


def solution(mesh):
    return jax.shard_map(
        shards,
        mesh=mesh,
        in_specs=(
            P(("row", "col"), None),
            P("row", "col", None, None, None),
            P("row", "col", None),
            P("row", "col", None),
            P("row", "col"),
        ),
        out_specs=(P(("row", "col"), None), P(("row", "col"), None)),
        check_vma=False,
    )
```

```python
import functools

import jax
import jax.numpy as jnp
from jax import lax
from jax.experimental import pallas as pl
from jax.experimental.pallas import tpu as pltpu
from jax.sharding import PartitionSpec as P

NX, NYH, NCORE, NZ, NYL = 4, 2, 2, 8, 2
TILE = 128
OWN = 2
EXTRA = 8
UNROLL = 8
TERMS = 3


def row_shift(value, dx=0, dyh=0, dcore=0):
    pairs = []
    for r in range(NX * NYH * NCORE):
        x, yh, core = r // 4, (r // 2) % 2, r % 2
        pairs.append((r, ((x + dx) % NX) * 4 + (yh ^ dyh) * 2 + (core ^ dcore)))
    return lax.ppermute(value, "row", pairs)


def col_shift(value, dz=0, dyl=0):
    pairs = []
    for c in range(NZ * NYL):
        z, yl = c // 2, c % 2
        pairs.append((c, ((z + dz) % NZ) * 2 + (yl ^ dyl)))
    return lax.ppermute(value, "col", pairs)


def gather_row(shard):
    pair = jnp.stack([shard, row_shift(shard, dyh=1)])
    near = [pair] + [row_shift(pair, dx=d) for d in (1, 2, 3)]
    return near + [row_shift(piece, dcore=1) for piece in near]


def scatter_row(parts):
    near = [parts[d] + row_shift(parts[NX + d], dcore=1) for d in range(NX)]
    total = near[0]
    for d in (1, 2, 3):
        total = total + row_shift(near[d], dx=d)
    return total[0] + row_shift(total[1], dyh=1)


def gather_col(shard):
    pair = jnp.stack([shard, col_shift(shard, dyl=1)])
    pieces = [pair] * NZ
    up = down = pair
    for d in (1, 2, 3, 4):
        up = col_shift(up, dz=1)
        pieces[d] = up
        if d < 4:
            down = col_shift(down, dz=-1)
            pieces[NZ - d] = down
    return pieces


def scatter_col(parts):
    up = col_shift(parts[4], dz=1) + parts[3]
    down = col_shift(parts[5], dz=-1) + parts[6]
    up = col_shift(up, dz=1) + parts[2]
    down = col_shift(down, dz=-1) + parts[7]
    up = col_shift(up, dz=1) + parts[1]
    down = col_shift(down, dz=-1)
    up = col_shift(up, dz=1)
    total = parts[0] + up + down
    return total[0] + col_shift(total[1], dyl=1)


def split_into(split_ref, block, value):
    for term in range(TERMS):
        part = value.astype(jnp.bfloat16)
        split_ref[block, :, term * TILE : (term + 1) * TILE] = part
        if term + 1 < TERMS:
            value = value - part.astype(jnp.float32)


def sum_groups(value):
    return jnp.sum(value.reshape(-1, EXTRA, TILE), axis=0)


def mirrored_piece(p):
    return (p // NX) * NX + (NX - p % NX) % NX


def product_kernel(piece_count, paired_count, first, contract, rows, *refs):
    source_ref, target_ref, tiles_ref = refs[:3]
    piece_refs = refs[3 : 3 + piece_count]
    paired_refs = refs[3 + piece_count : 3 + piece_count + paired_count]
    out_refs = refs[3 + piece_count + paired_count : -2]
    split_ref, total_ref = refs[-2:]
    slots = tiles_ref.shape[0]
    pieces = [piece.at[q] for piece in piece_refs for q in range(piece.shape[0])]
    outs = [out.at[q] for out in out_refs for q in range(out.shape[0])]
    for p, piece in enumerate(pieces):
        for h in range(OWN):
            split_into(split_ref, p * OWN + h, piece[h * TILE : (h + 1) * TILE, :])
    total_ref[...] = jnp.zeros_like(total_ref)

    def block_product(k):
        product = lax.dot_general(
            tiles_ref[k],
            split_ref[source_ref[k]],
            (((contract,), (0,)), ((), ())),
            preferred_element_type=jnp.float32,
        )
        added = product[:, :TILE]
        for term in range(1, TERMS):
            added = added + product[:, term * TILE : (term + 1) * TILE]
        return added

    def one(k):
        total_ref[target_ref[k]] += block_product(k)

    head = first + (slots - first) % UNROLL
    for k in range(first, head):
        one(k)

    def body(step, carry):
        for u in range(UNROLL):
            one(head + step * UNROLL + u)
        return carry

    lax.fori_loop(0, (slots - head) // UNROLL, body, 0)
    if paired_count:
        extra = jnp.zeros((EXTRA, TILE), jnp.float32)
        for p in range(len(outs)):
            paired = paired_refs[mirrored_piece(p // NYH)].at[p % NYH]
            for h in range(OWN):
                extra = extra + sum_groups(paired[h * TILE : (h + 1) * TILE, :] * total_ref[p * OWN + h])
        extra = extra + extra
        for k in range(OWN):
            extra = extra + sum_groups(pieces[0][k * TILE : (k + 1) * TILE, :] * block_product(k))
    elif rows > OWN * TILE:
        extra = pieces[0][OWN * TILE :, :]
        for piece in pieces[1:]:
            extra = extra + piece[OWN * TILE :, :]
    for p, out in enumerate(outs):
        for h in range(OWN):
            out[h * TILE : (h + 1) * TILE, :] = total_ref[p * OWN + h]
        if rows > OWN * TILE:
            out[OWN * TILE :, :] = extra


def products(sources, targets, tiles, pieces, paired, sizes, first, contract, rows):
    count = sum(sizes)
    smem = pl.BlockSpec(memory_space=pltpu.SMEM)
    vmem = pl.BlockSpec(memory_space=pltpu.VMEM)
    return pl.pallas_call(
        functools.partial(product_kernel, len(pieces), len(paired), first, contract, rows),
        out_shape=[jax.ShapeDtypeStruct((size, rows, TILE), jnp.float32) for size in sizes],
        in_specs=[smem, smem] + [vmem] * (1 + len(pieces) + len(paired)),
        out_specs=[vmem] * len(sizes),
        scratch_shapes=[
            pltpu.VMEM((count * OWN, TILE, TERMS * TILE), jnp.bfloat16),
            pltpu.VMEM((count * OWN + 1, TILE, TILE), jnp.float32),
        ],
        compiler_params=pltpu.CompilerParams(vmem_limit_bytes=32 * 1024 * 1024),
        cost_estimate=pl.CostEstimate(
            flops=tiles.shape[0] * 2 * TERMS * TILE**3, bytes_accessed=6 * 1024 * 1024, transcendentals=0
        ),
    )(sources, targets, tiles, *pieces, *paired)


def places(row_blocks, col_blocks, block_counts):
    slots = row_blocks.shape[-1]
    row_blocks = row_blocks.reshape(slots)
    col_blocks = col_blocks.reshape(slots)
    r, c = lax.axis_index("row"), lax.axis_index("col")
    x, yh, core = r // 4, (r // 2) % 2, r % 2
    z, yl = c // 2, c % 2
    slot = jnp.arange(slots, dtype=jnp.int32)
    live = slot < block_counts.reshape(())
    device, half = col_blocks // OWN, col_blocks % OWN
    dcore, dyh, ox = core ^ (device % 2), yh ^ ((device // 2) % 2), device // 4
    direct_source = ((dcore * NX + (x - ox) % NX) * NYH + dyh) * OWN + half
    mirror_target = ((dcore * NX + (ox - x) % NX) * NYH + dyh) * OWN + half
    device, half = row_blocks // OWN, row_blocks % OWN
    dyl, oz = yl ^ (device % 2), device // 2
    mirror_source = (((z - oz) % NZ) * NYL + dyl) * OWN + half
    direct_target = (((oz - z) % NZ) * NYL + dyl) * OWN + half
    unused = NX * NYH * NCORE * OWN
    direct_target = jnp.where(live, direct_target, unused)
    mirror_target = jnp.where(live & (slot >= OWN), mirror_target, unused)
    return direct_source, direct_target, mirror_source, mirror_target


def apply_matrix(vector, sums, tiles, where, energy=False):
    direct_source, direct_target, mirror_source, mirror_target = where
    own = vector.shape[0]
    by_row = gather_row(jnp.concatenate([vector, sums]))
    by_col = gather_col(vector)
    direct = products(direct_source, direct_target, tiles, by_row, [], (NYL,) * NZ, 0, 1, own + EXTRA)
    paired, rows = (by_row, own + EXTRA) if energy else ([], own)
    sizes = (NYH,) * (NX * NCORE)
    mirror = products(mirror_source, mirror_target, tiles, by_col, paired, sizes, OWN, 0, rows)
    image = scatter_col(direct)
    mirror_image = scatter_row(mirror)
    return image[:own] + mirror_image[:own], image[own:], mirror_image[own:]


def column_dots(pairs):
    dots = jnp.stack([jnp.sum(a * b, axis=0) for a, b in pairs])
    return jnp.concatenate([dots, jnp.zeros((EXTRA - len(pairs), dots.shape[1]), jnp.float32)])


def sum_col(value):
    devices = NZ * NYL
    parts = lax.all_to_all(jnp.broadcast_to(value, (devices, *value.shape)), "col", 0, 0, tiled=True)
    return jnp.sum(parts, axis=(0, 1))


def shards(right_side, cov_blocks, row_blocks, col_blocks, block_counts):
    tiles = cov_blocks.reshape(cov_blocks.shape[2:])
    where = places(row_blocks, col_blocks, block_counts)
    apply = functools.partial(apply_matrix, tiles=tiles, where=where)
    live = jnp.arange(tiles.shape[0], dtype=jnp.int32) < block_counts.reshape(())
    largest = jnp.max(jnp.where(live, jnp.max(jnp.abs(tiles), axis=(1, 2)).astype(jnp.float32), 0.0))

    r0 = right_side
    w0, sums, _ = apply(r0, jnp.full((EXTRA, r0.shape[1]), largest, jnp.float32))
    scale = 256.0 / sums[:1]
    w0 = scale * w0
    z0, sums, _ = apply(w0, column_dots([(r0, r0), (w0, r0)]))
    z0 = scale * z0
    norm0, curvature = sums[0], sums[1]
    alpha0 = norm0 / curvature
    r1 = r0 - alpha0 * w0
    w1 = w0 - alpha0 * z0
    pairs = [(r1, r1), (r1, w1), (w1, w1), (r1, w0), (w1, w0), (w0, w0), (w1, z0), (w0, z0)]
    q1, sums, energy = apply(w1, column_dots(pairs), energy=True)
    q1 = scale * q1
    energy = scale[0] * sum_col(energy)
    norm1, r1w1, w1w1, r1w0, w1w0, w0w0, w1z0, w0z0 = [sums[n] for n in range(EXTRA)]
    beta1 = norm1 / norm0
    alpha1 = norm1 / (r1w1 - beta1 * norm1 / alpha0)
    r1s1 = r1w1 + beta1 * r1w0
    w1s1 = w1w1 + beta1 * w1w0
    s1s1 = w1s1 + beta1 * (w1w0 + beta1 * w0w0)
    s1z1 = energy + beta1 * (2.0 * w1z0 + beta1 * w0z0)
    norm2 = norm1 - alpha1 * (2.0 * r1s1 - alpha1 * s1s1)
    r2w2 = r1w1 - alpha1 * (2.0 * w1s1 - alpha1 * s1z1)
    beta2 = norm2 / norm1
    alpha2 = norm2 / (r2w2 - beta2 * norm2 / alpha1)
    p1 = r1 + beta1 * r0
    s1 = w1 + beta1 * w0
    z1 = q1 + beta1 * z0
    r2 = r1 - alpha1 * s1
    w2 = w1 - alpha1 * z1
    solution_field = scale * (alpha0 * r0 + alpha1 * p1 + alpha2 * (r2 + beta2 * p1))
    residual = r2 - alpha2 * (w2 + beta2 * s1)
    return (solution_field, residual)


def solution(mesh):
    return jax.shard_map(
        shards,
        mesh=mesh,
        in_specs=(
            P(("row", "col"), None),
            P("row", "col", None, None, None),
            P("row", "col", None),
            P("row", "col", None),
            P("row", "col"),
        ),
        out_specs=(P(("row", "col"), None), P(("row", "col"), None)),
        check_vma=False,
    )
```

```python
import functools

import jax
import jax.numpy as jnp
from jax import lax
from jax.experimental import pallas as pl
from jax.experimental.pallas import tpu as pltpu
from jax.sharding import PartitionSpec as P

NX, NYH, NCORE, NZ, NYL = 4, 2, 2, 8, 2
TILE = 128
OWN = 2
EXTRA = 8
TERMS = 3


def row_shift(value, dx=0, dyh=0, dcore=0):
    pairs = []
    for r in range(NX * NYH * NCORE):
        x, yh, core = r // 4, (r // 2) % 2, r % 2
        pairs.append((r, ((x + dx) % NX) * 4 + (yh ^ dyh) * 2 + (core ^ dcore)))
    return lax.ppermute(value, "row", pairs)


def col_shift(value, dz=0, dyl=0):
    pairs = []
    for c in range(NZ * NYL):
        z, yl = c // 2, c % 2
        pairs.append((c, ((z + dz) % NZ) * 2 + (yl ^ dyl)))
    return lax.ppermute(value, "col", pairs)


def gather_row(shard):
    pair = jnp.stack([shard, row_shift(shard, dyh=1)])
    near = [pair] + [row_shift(pair, dx=d) for d in (1, 2, 3)]
    return near + [row_shift(piece, dcore=1) for piece in near]


def scatter_row(parts):
    near = [parts[d] + row_shift(parts[NX + d], dcore=1) for d in range(NX)]
    total = near[0]
    for d in (1, 2, 3):
        total = total + row_shift(near[d], dx=d)
    return total[0] + row_shift(total[1], dyh=1)


def gather_col(shard):
    pair = jnp.stack([shard, col_shift(shard, dyl=1)])
    pieces = [pair] * NZ
    up = down = pair
    for d in (1, 2, 3, 4):
        up = col_shift(up, dz=1)
        pieces[d] = up
        if d < 4:
            down = col_shift(down, dz=-1)
            pieces[NZ - d] = down
    return pieces


def scatter_col(parts):
    up = col_shift(parts[4], dz=1) + parts[3]
    down = col_shift(parts[5], dz=-1) + parts[6]
    up = col_shift(up, dz=1) + parts[2]
    down = col_shift(down, dz=-1) + parts[7]
    up = col_shift(up, dz=1) + parts[1]
    down = col_shift(down, dz=-1)
    up = col_shift(up, dz=1)
    total = parts[0] + up + down
    return total[0] + col_shift(total[1], dyl=1)


def split_into(split_ref, block, value):
    for term in range(TERMS):
        part = value.astype(jnp.bfloat16)
        split_ref[block, term * TILE : (term + 1) * TILE, :] = part
        if term + 1 < TERMS:
            value = value - part.astype(jnp.float32)


def sum_groups(value):
    return jnp.sum(value.reshape(-1, EXTRA, TILE), axis=0)


def mirrored_piece(p):
    return (p // NX) * NX + (NX - p % NX) % NX


def product_kernel(piece_count, paired_count, first, contract, rows, *refs):
    source_ref, target_ref, tiles_ref = refs[:3]
    piece_refs = refs[3 : 3 + piece_count]
    paired_refs = refs[3 + piece_count : 3 + piece_count + paired_count]
    out_refs = refs[3 + piece_count + paired_count : -2]
    split_ref, total_ref = refs[-2:]
    slots = tiles_ref.shape[0]
    pieces = [piece.at[q] for piece in piece_refs for q in range(piece.shape[0])]
    outs = [out.at[q] for out in out_refs for q in range(out.shape[0])]
    for p, piece in enumerate(pieces):
        for h in range(OWN):
            split_into(split_ref, p * OWN + h, piece[h * TILE : (h + 1) * TILE, :])
    total_ref[...] = jnp.zeros_like(total_ref)

    def block_product(k):
        tile = tiles_ref[k] if contract else tiles_ref[k].T
        return jnp.dot(
            jnp.concatenate([tile] * TERMS, axis=1), split_ref[source_ref[k]], preferred_element_type=jnp.float32
        )

    def one(k):
        total_ref[target_ref[k]] += block_product(k)

    for k in range(first, slots):
        one(k)
    if paired_count:
        extra = jnp.zeros((EXTRA, TILE), jnp.float32)
        for p in range(len(outs)):
            paired = paired_refs[mirrored_piece(p // NYH)].at[p % NYH]
            for h in range(OWN):
                extra = extra + sum_groups(paired[h * TILE : (h + 1) * TILE, :] * total_ref[p * OWN + h])
        extra = extra + extra
        for k in range(OWN):
            extra = extra + sum_groups(pieces[0][k * TILE : (k + 1) * TILE, :] * block_product(k))
    elif rows > OWN * TILE:
        extra = pieces[0][OWN * TILE :, :]
        for piece in pieces[1:]:
            extra = extra + piece[OWN * TILE :, :]
    for p, out in enumerate(outs):
        for h in range(OWN):
            out[h * TILE : (h + 1) * TILE, :] = total_ref[p * OWN + h]
        if rows > OWN * TILE:
            out[OWN * TILE :, :] = extra


def products(sources, targets, tiles, pieces, paired, sizes, first, contract, rows):
    count = sum(sizes)
    smem = pl.BlockSpec(memory_space=pltpu.SMEM)
    vmem = pl.BlockSpec(memory_space=pltpu.VMEM)
    return pl.pallas_call(
        functools.partial(product_kernel, len(pieces), len(paired), first, contract, rows),
        out_shape=[jax.ShapeDtypeStruct((size, rows, TILE), jnp.float32) for size in sizes],
        in_specs=[smem, smem] + [vmem] * (1 + len(pieces) + len(paired)),
        out_specs=[vmem] * len(sizes),
        scratch_shapes=[
            pltpu.VMEM((count * OWN, TERMS * TILE, TILE), jnp.bfloat16),
            pltpu.VMEM((count * OWN + 1, TILE, TILE), jnp.float32),
        ],
        compiler_params=pltpu.CompilerParams(vmem_limit_bytes=32 * 1024 * 1024),
        cost_estimate=pl.CostEstimate(
            flops=tiles.shape[0] * 2 * TERMS * TILE**3, bytes_accessed=6 * 1024 * 1024, transcendentals=0
        ),
    )(sources, targets, tiles, *pieces, *paired)


def places(row_blocks, col_blocks, block_counts):
    slots = row_blocks.shape[-1]
    row_blocks = row_blocks.reshape(slots)
    col_blocks = col_blocks.reshape(slots)
    r, c = lax.axis_index("row"), lax.axis_index("col")
    x, yh, core = r // 4, (r // 2) % 2, r % 2
    z, yl = c // 2, c % 2
    slot = jnp.arange(slots, dtype=jnp.int32)
    live = slot < block_counts.reshape(())
    device, half = col_blocks // OWN, col_blocks % OWN
    dcore, dyh, ox = core ^ (device % 2), yh ^ ((device // 2) % 2), device // 4
    direct_source = ((dcore * NX + (x - ox) % NX) * NYH + dyh) * OWN + half
    mirror_target = ((dcore * NX + (ox - x) % NX) * NYH + dyh) * OWN + half
    device, half = row_blocks // OWN, row_blocks % OWN
    dyl, oz = yl ^ (device % 2), device // 2
    mirror_source = (((z - oz) % NZ) * NYL + dyl) * OWN + half
    direct_target = (((oz - z) % NZ) * NYL + dyl) * OWN + half
    unused = NX * NYH * NCORE * OWN
    direct_target = jnp.where(live, direct_target, unused)
    mirror_target = jnp.where(live & (slot >= OWN), mirror_target, unused)
    return direct_source, direct_target, mirror_source, mirror_target


def apply_matrix(vector, sums, tiles, where, energy=False):
    direct_source, direct_target, mirror_source, mirror_target = where
    own = vector.shape[0]
    by_row = gather_row(jnp.concatenate([vector, sums]))
    by_col = gather_col(vector)
    direct = products(direct_source, direct_target, tiles, by_row, [], (NYL,) * NZ, 0, 1, own + EXTRA)
    paired, rows = (by_row, own + EXTRA) if energy else ([], own)
    sizes = (NYH,) * (NX * NCORE)
    mirror = products(mirror_source, mirror_target, tiles, by_col, paired, sizes, OWN, 0, rows)
    image = scatter_col(direct)
    mirror_image = scatter_row(mirror)
    return image[:own] + mirror_image[:own], image[own:], mirror_image[own:]


def column_dots(pairs):
    dots = jnp.stack([jnp.sum(a * b, axis=0) for a, b in pairs])
    return jnp.concatenate([dots, jnp.zeros((EXTRA - len(pairs), dots.shape[1]), jnp.float32)])


def sum_col(value):
    devices = NZ * NYL
    parts = lax.all_to_all(jnp.broadcast_to(value, (devices, *value.shape)), "col", 0, 0, tiled=True)
    return jnp.sum(parts, axis=(0, 1))


def shards(right_side, cov_blocks, row_blocks, col_blocks, block_counts):
    tiles = cov_blocks.reshape(cov_blocks.shape[2:])
    where = places(row_blocks, col_blocks, block_counts)
    apply = functools.partial(apply_matrix, tiles=tiles, where=where)
    live = jnp.arange(tiles.shape[0], dtype=jnp.int32) < block_counts.reshape(())
    largest = jnp.max(jnp.where(live, jnp.max(jnp.abs(tiles), axis=(1, 2)).astype(jnp.float32), 0.0))

    r0 = right_side
    w0, sums, _ = apply(r0, jnp.full((EXTRA, r0.shape[1]), largest, jnp.float32))
    scale = 256.0 / sums[:1]
    w0 = scale * w0
    z0, sums, _ = apply(w0, column_dots([(r0, r0), (w0, r0)]))
    z0 = scale * z0
    norm0, curvature = sums[0], sums[1]
    alpha0 = norm0 / curvature
    r1 = r0 - alpha0 * w0
    w1 = w0 - alpha0 * z0
    pairs = [(r1, r1), (r1, w1), (w1, w1), (r1, w0), (w1, w0), (w0, w0), (w1, z0), (w0, z0)]
    q1, sums, energy = apply(w1, column_dots(pairs), energy=True)
    q1 = scale * q1
    energy = scale[0] * sum_col(energy)
    norm1, r1w1, w1w1, r1w0, w1w0, w0w0, w1z0, w0z0 = [sums[n] for n in range(EXTRA)]
    beta1 = norm1 / norm0
    alpha1 = norm1 / (r1w1 - beta1 * norm1 / alpha0)
    r1s1 = r1w1 + beta1 * r1w0
    w1s1 = w1w1 + beta1 * w1w0
    s1s1 = w1s1 + beta1 * (w1w0 + beta1 * w0w0)
    s1z1 = energy + beta1 * (2.0 * w1z0 + beta1 * w0z0)
    norm2 = norm1 - alpha1 * (2.0 * r1s1 - alpha1 * s1s1)
    r2w2 = r1w1 - alpha1 * (2.0 * w1s1 - alpha1 * s1z1)
    beta2 = norm2 / norm1
    alpha2 = norm2 / (r2w2 - beta2 * norm2 / alpha1)
    p1 = r1 + beta1 * r0
    s1 = w1 + beta1 * w0
    z1 = q1 + beta1 * z0
    r2 = r1 - alpha1 * s1
    w2 = w1 - alpha1 * z1
    solution_field = scale * (alpha0 * r0 + alpha1 * p1 + alpha2 * (r2 + beta2 * p1))
    residual = r2 - alpha2 * (w2 + beta2 * s1)
    return (solution_field, residual)


def solution(mesh):
    return jax.shard_map(
        shards,
        mesh=mesh,
        in_specs=(
            P(("row", "col"), None),
            P("row", "col", None, None, None),
            P("row", "col", None),
            P("row", "col", None),
            P("row", "col"),
        ),
        out_specs=(P(("row", "col"), None), P(("row", "col"), None)),
        check_vma=False,
    )
```

```python
import functools

import jax
import jax.numpy as jnp
from jax import lax
from jax.experimental import pallas as pl
from jax.experimental.pallas import tpu as pltpu
from jax.sharding import PartitionSpec as P

NX, NYH, NCORE, NZ, NYL = 4, 2, 2, 8, 2
TILE = 128
OWN = 2
EXTRA = 8
TERMS = 3


def row_shift(value, dx=0, dyh=0, dcore=0):
    pairs = []
    for r in range(NX * NYH * NCORE):
        x, yh, core = r // 4, (r // 2) % 2, r % 2
        pairs.append((r, ((x + dx) % NX) * 4 + (yh ^ dyh) * 2 + (core ^ dcore)))
    return lax.ppermute(value, "row", pairs)


def col_shift(value, dz=0, dyl=0):
    pairs = []
    for c in range(NZ * NYL):
        z, yl = c // 2, c % 2
        pairs.append((c, ((z + dz) % NZ) * 2 + (yl ^ dyl)))
    return lax.ppermute(value, "col", pairs)


def gather_row(shard):
    pair = jnp.stack([shard, row_shift(shard, dyh=1)])
    near = [pair] + [row_shift(pair, dx=d) for d in (1, 2, 3)]
    return near + [row_shift(piece, dcore=1) for piece in near]


def scatter_row(parts):
    near = [parts[d] + row_shift(parts[NX + d], dcore=1) for d in range(NX)]
    total = near[0]
    for d in (1, 2, 3):
        total = total + row_shift(near[d], dx=d)
    return total[0] + row_shift(total[1], dyh=1)


def gather_col(shard):
    pair = jnp.stack([shard, col_shift(shard, dyl=1)])
    pieces = [pair] * NZ
    up = down = pair
    for d in (1, 2, 3, 4):
        up = col_shift(up, dz=1)
        pieces[d] = up
        if d < 4:
            down = col_shift(down, dz=-1)
            pieces[NZ - d] = down
    return pieces


def scatter_col(parts):
    up = col_shift(parts[4], dz=1) + parts[3]
    down = col_shift(parts[5], dz=-1) + parts[6]
    up = col_shift(up, dz=1) + parts[2]
    down = col_shift(down, dz=-1) + parts[7]
    up = col_shift(up, dz=1) + parts[1]
    down = col_shift(down, dz=-1)
    up = col_shift(up, dz=1)
    total = parts[0] + up + down
    return total[0] + col_shift(total[1], dyl=1)


def split_into(split_ref, block, value):
    for term in range(TERMS):
        part = value.astype(jnp.bfloat16)
        split_ref[block, term * TILE : (term + 1) * TILE, :] = part
        if term + 1 < TERMS:
            value = value - part.astype(jnp.float32)


def sum_groups(value):
    return jnp.sum(value.reshape(-1, EXTRA, TILE), axis=0)


def mirrored_piece(p):
    return (p // NX) * NX + (NX - p % NX) % NX


def product_kernel(piece_count, paired_count, first, contract, rows, *refs):
    source_ref, target_ref, tiles_ref = refs[:3]
    piece_refs = refs[3 : 3 + piece_count]
    paired_refs = refs[3 + piece_count : 3 + piece_count + paired_count]
    out_refs = refs[3 + piece_count + paired_count : -2]
    split_ref, total_ref = refs[-2:]
    slots = tiles_ref.shape[0]
    pieces = [piece.at[q] for piece in piece_refs for q in range(piece.shape[0])]
    outs = [out.at[q] for out in out_refs for q in range(out.shape[0])]
    for p, piece in enumerate(pieces):
        for h in range(OWN):
            split_into(split_ref, p * OWN + h, piece[h * TILE : (h + 1) * TILE, :])
    total_ref[...] = jnp.zeros_like(total_ref)

    def block_product(k):
        tile = tiles_ref[k] if contract else tiles_ref[k].T
        return jnp.dot(
            jnp.concatenate([tile] * TERMS, axis=1), split_ref[source_ref[k]], preferred_element_type=jnp.float32
        )

    def one(k):
        total_ref[target_ref[k]] += block_product(k)

    for k in range(first, slots):
        one(k)
    if paired_count:
        extra = jnp.zeros((EXTRA, TILE), jnp.float32)
        for p in range(len(outs)):
            paired = paired_refs[mirrored_piece(p // NYH)].at[p % NYH]
            for h in range(OWN):
                extra = extra + sum_groups(paired[h * TILE : (h + 1) * TILE, :] * total_ref[p * OWN + h])
        extra = extra + extra
        for k in range(OWN):
            extra = extra + sum_groups(pieces[0][k * TILE : (k + 1) * TILE, :] * block_product(k))
    elif rows > OWN * TILE:
        extra = pieces[0][OWN * TILE :, :]
        for piece in pieces[1:]:
            extra = extra + piece[OWN * TILE :, :]
    for p, out in enumerate(outs):
        for h in range(OWN):
            out[h * TILE : (h + 1) * TILE, :] = total_ref[p * OWN + h]
        if rows > OWN * TILE:
            out[OWN * TILE :, :] = extra


def products(sources, targets, tiles, pieces, paired, sizes, first, contract, rows):
    count = sum(sizes)
    smem = pl.BlockSpec(memory_space=pltpu.SMEM)
    vmem = pl.BlockSpec(memory_space=pltpu.VMEM)
    return pl.pallas_call(
        functools.partial(product_kernel, len(pieces), len(paired), first, contract, rows),
        out_shape=[jax.ShapeDtypeStruct((size, rows, TILE), jnp.float32) for size in sizes],
        in_specs=[smem, smem] + [vmem] * (1 + len(pieces) + len(paired)),
        out_specs=[vmem] * len(sizes),
        scratch_shapes=[
            pltpu.VMEM((count * OWN, TERMS * TILE, TILE), jnp.bfloat16),
            pltpu.VMEM((count * OWN + 1, TILE, TILE), jnp.float32),
        ],
        compiler_params=pltpu.CompilerParams(vmem_limit_bytes=32 * 1024 * 1024),
        cost_estimate=pl.CostEstimate(
            flops=tiles.shape[0] * 2 * TERMS * TILE**3, bytes_accessed=6 * 1024 * 1024, transcendentals=0
        ),
    )(sources, targets, tiles, *pieces, *paired)


def places(row_blocks, col_blocks, block_counts):
    slots = row_blocks.shape[-1]
    row_blocks = row_blocks.reshape(slots)
    col_blocks = col_blocks.reshape(slots)
    r, c = lax.axis_index("row"), lax.axis_index("col")
    x, yh, core = r // 4, (r // 2) % 2, r % 2
    z, yl = c // 2, c % 2
    slot = jnp.arange(slots, dtype=jnp.int32)
    live = slot < block_counts.reshape(())
    device, half = col_blocks // OWN, col_blocks % OWN
    dcore, dyh, ox = core ^ (device % 2), yh ^ ((device // 2) % 2), device // 4
    direct_source = ((dcore * NX + (x - ox) % NX) * NYH + dyh) * OWN + half
    mirror_target = ((dcore * NX + (ox - x) % NX) * NYH + dyh) * OWN + half
    device, half = row_blocks // OWN, row_blocks % OWN
    dyl, oz = yl ^ (device % 2), device // 2
    mirror_source = (((z - oz) % NZ) * NYL + dyl) * OWN + half
    direct_target = (((oz - z) % NZ) * NYL + dyl) * OWN + half
    unused = NX * NYH * NCORE * OWN
    direct_target = jnp.where(live, direct_target, unused)
    mirror_target = jnp.where(live & (slot >= OWN), mirror_target, unused)
    return direct_source, direct_target, mirror_source, mirror_target


def apply_matrix(vector, sums, tiles, where, energy=False):
    direct_source, direct_target, mirror_source, mirror_target = where
    own = vector.shape[0]
    by_row = gather_row(jnp.concatenate([vector, sums]))
    by_col = gather_col(vector)
    direct = products(direct_source, direct_target, tiles, by_row, [], (NYL,) * NZ, 0, 1, own + EXTRA)
    paired, rows = (by_row, own + EXTRA) if energy else ([], own)
    sizes = (NYH,) * (NX * NCORE)
    mirror = products(mirror_source, mirror_target, tiles, by_col, paired, sizes, OWN, 0, rows)
    image = scatter_col(direct)
    mirror_image = scatter_row(mirror)
    return image[:own] + mirror_image[:own], image[own:], mirror_image[own:]


def column_dots(pairs):
    dots = jnp.stack([jnp.sum(a * b, axis=0) for a, b in pairs])
    return jnp.concatenate([dots, jnp.zeros((EXTRA - len(pairs), dots.shape[1]), jnp.float32)])


def sum_col(value):
    devices = NZ * NYL
    parts = lax.all_to_all(jnp.broadcast_to(value, (devices, *value.shape)), "col", 0, 0, tiled=True)
    return jnp.sum(parts, axis=(0, 1))


def shards(right_side, cov_blocks, row_blocks, col_blocks, block_counts):
    tiles = cov_blocks.reshape(cov_blocks.shape[2:])
    where = places(row_blocks, col_blocks, block_counts)
    apply = functools.partial(apply_matrix, tiles=tiles, where=where)
    live = (jnp.arange(tiles.shape[0], dtype=jnp.int32) < block_counts.reshape(()))[:, None, None]
    largest = jnp.max(jnp.max(jnp.where(live, jnp.abs(tiles), 0).astype(jnp.float32), axis=0))

    r0 = right_side
    w0, sums, _ = apply(r0, jnp.full((EXTRA, r0.shape[1]), largest, jnp.float32))
    scale = 256.0 / sums[:1]
    w0 = scale * w0
    z0, sums, _ = apply(w0, column_dots([(r0, r0), (w0, r0)]))
    z0 = scale * z0
    norm0, curvature = sums[0], sums[1]
    alpha0 = norm0 / curvature
    r1 = r0 - alpha0 * w0
    w1 = w0 - alpha0 * z0
    pairs = [(r1, r1), (r1, w1), (w1, w1), (r1, w0), (w1, w0), (w0, w0), (w1, z0), (w0, z0)]
    q1, sums, energy = apply(w1, column_dots(pairs), energy=True)
    q1 = scale * q1
    energy = scale[0] * sum_col(energy)
    norm1, r1w1, w1w1, r1w0, w1w0, w0w0, w1z0, w0z0 = [sums[n] for n in range(EXTRA)]
    beta1 = norm1 / norm0
    alpha1 = norm1 / (r1w1 - beta1 * norm1 / alpha0)
    r1s1 = r1w1 + beta1 * r1w0
    w1s1 = w1w1 + beta1 * w1w0
    s1s1 = w1s1 + beta1 * (w1w0 + beta1 * w0w0)
    s1z1 = energy + beta1 * (2.0 * w1z0 + beta1 * w0z0)
    norm2 = norm1 - alpha1 * (2.0 * r1s1 - alpha1 * s1s1)
    r2w2 = r1w1 - alpha1 * (2.0 * w1s1 - alpha1 * s1z1)
    beta2 = norm2 / norm1
    alpha2 = norm2 / (r2w2 - beta2 * norm2 / alpha1)
    p1 = r1 + beta1 * r0
    s1 = w1 + beta1 * w0
    z1 = q1 + beta1 * z0
    r2 = r1 - alpha1 * s1
    w2 = w1 - alpha1 * z1
    solution_field = scale * (alpha0 * r0 + alpha1 * p1 + alpha2 * (r2 + beta2 * p1))
    residual = r2 - alpha2 * (w2 + beta2 * s1)
    return (solution_field, residual)


def solution(mesh):
    return jax.shard_map(
        shards,
        mesh=mesh,
        in_specs=(
            P(("row", "col"), None),
            P("row", "col", None, None, None),
            P("row", "col", None),
            P("row", "col", None),
            P("row", "col"),
        ),
        out_specs=(P(("row", "col"), None), P(("row", "col"), None)),
        check_vma=False,
    )
```
